512 devices in a mesh: dp: 64 (over y, x, core), tensor: 8 (over z).
Axes of the slice: x: 4, y: 8, z: 8, core: 2. Of those that a mesh axis runs over, the one named last changes fastest.
Arguments:
- features: bfloat16 [16384, 8192], P('dp', 'tensor'), may hold values from -6 to 6
- gate_pre: bfloat16 [16384, 14336], P('dp', 'tensor'), may hold values from -6 to 6
- up_pre: bfloat16 [16384, 14336], P('dp', 'tensor'), may hold values from -6 to 6
- grad_hidden: bfloat16 [16384, 14336], P('dp', 'tensor'), may hold values from -0.4375 to 0.4375
- blocks: int32 [512, 3], P('tensor'), may hold values from 0 to 63, as said below
- owner: int32 [512], P('tensor'), may hold values from 0 to 63, as said below
- weights: float32 [1536, 128, 128], P(('dp', 'tensor')), may hold values from -0.4375 to 0.4375
- moment1: float32 [1536, 128, 128], P(('dp', 'tensor')), may hold values from -6 to 6
- moment2: float32 [1536, 128, 128], P(('dp', 'tensor')), may hold values from 0.05 to 2
Outputs:
- new_weights: float32 [1536, 128, 128], P(('dp', 'tensor'))
- new_moment1: float32 [1536, 128, 128], P(('dp', 'tensor'))
- new_moment2: float32 [1536, 128, 128], P(('dp', 'tensor'))
The draws below stay inside these ranges and needn't reach their ends.
Inputs may be any that keep to these rules, and one draw needn't show every extreme that they name: Each row is (matrix, row block, column block): matrix 0 is the gate and 1 the up projection, row block below 64, column block below 14 and counted within the tensor index's own columns. The rows of one tensor index's list are distinct; columns hold unequal numbers of blocks. `owner`: in each tensor index's list no index of dp owns more than 3 blocks, and some index of dp owns exactly 3.
All inputs are finite; a program needn't handle non-finite values.
Results may differ from the reference program's by a relative error of at most 0.0028.
Values may be sent and summed in bfloat16 or wider, within the bound.
A program may use at most 64 MiB of HBM per device.

```python
import math
import jax
import jax.numpy as jnp
from jax import lax

D = 8192
FF = 14336
BS = 128
CAP = 3
REPLICAS = 64
TENSORS = 8
TOKENS = 16384
NBT = 64
N_DP = 64
N_TENSOR = 8


def draw_blocks(key, part):
    row_count = D // BS
    col_count = FF // N_TENSOR // BS
    cell_count = 2 * row_count * col_count

    def one_list(subkey):
        first_key, second_key = jax.random.split(subkey)
        column_weight = jax.random.randint(first_key, (col_count,), 1, 9)
        base = jax.random.randint(second_key, (2, row_count, col_count), 0, 4096)
        score = (base * column_weight[None, None, :]).reshape(-1) * cell_count + jnp.arange(cell_count, dtype=jnp.int32)
        picked = lax.top_k(score, NBT)[1].astype(jnp.int32)
        matrix_id = picked // (row_count * col_count)
        row_id = picked // col_count % row_count
        col_id = picked % col_count
        return jnp.stack([matrix_id, row_id, col_id], axis=1)
    subkeys = jax.random.split(jax.random.fold_in(key, 11), N_TENSOR)
    return jax.vmap(one_list)(subkeys).reshape(N_TENSOR * NBT, 3).astype(jnp.int32)


def draw_owner(key, part):
    slot_total = N_DP * CAP

    def one_list(subkey):
        first_key, second_key, third_key = jax.random.split(subkey, 3)
        busiest = jax.random.randint(first_key, (), 0, N_DP)
        slots = jnp.arange(slot_total, dtype=jnp.int32)
        slot_owner = slots // CAP
        score = jax.random.randint(second_key, (slot_total,), 0, 1 << 20)
        ranking = jnp.where(slot_owner == busiest, slots, slot_total + score * slot_total + slots)
        picked = jnp.argsort(ranking, stable=True)[:NBT].astype(jnp.int32)
        owners = picked // CAP
        shuffle = jax.random.permutation(third_key, NBT)
        return owners[shuffle]
    subkeys = jax.random.split(jax.random.fold_in(key, 23), N_TENSOR)
    return jax.vmap(one_list)(subkeys).reshape(N_TENSOR * NBT).astype(jnp.int32)


def steps_of(stream_key, extent, cuts, low, top_value):
    gain, own = 1.0, jax.random.fold_in(stream_key, 6)
    for axis_at, parts in cuts:
        steps = jnp.exp(jax.random.uniform(jax.random.fold_in(own, axis_at), (parts,), jnp.float32, low / len(cuts), top_value / len(cuts)))
        gain = gain * jnp.repeat(steps, extent[axis_at] // parts).reshape([-1 if axis == axis_at else 1 for axis in range(len(extent))])
    return gain


def scatter_about(stream_key, extent, deviation, reach, cuts=(), kind=jnp.bfloat16):
    array = jax.random.normal(stream_key, extent, jnp.float32) * deviation
    if len(cuts) > 0:
        array = steps_of(stream_key, extent, cuts, -0.22, 0.18) * array
    return jnp.clip(array, min=-reach, max=reach).astype(kind)


def setup_inputs(seed: int = 0) -> dict:
    seeds = jax.random.split(jax.random.key(seed), 10)
    return {
        "features": scatter_about(seeds[0], (TOKENS, D), 1.0, 6.0, ((0, 64), (1, 8))),
        "gate_pre": scatter_about(seeds[1], (TOKENS, FF), 1.0, 6.0, ((0, 64), (1, 8))),
        "up_pre": scatter_about(seeds[2], (TOKENS, FF), 1.0, 6.0, ((0, 64), (1, 8))),
        "grad_hidden": scatter_about(seeds[3], (TOKENS, FF), 0.03, 0.4375, ((0, 64), (1, 8))),
        "blocks": draw_blocks(jax.random.fold_in(seeds[9], 71), 0),
        "owner": draw_owner(jax.random.fold_in(seeds[9], 71), 0),
        "weights": scatter_about(seeds[6], (REPLICAS * TENSORS * CAP, BS, BS), 0.03, 0.4375, ((0, 512),), jnp.float32),
        "moment1": scatter_about(seeds[7], (REPLICAS * TENSORS * CAP, BS, BS), 0.5, 6.0, ((0, 512),), jnp.float32),
        "moment2": jnp.clip(jnp.exp(math.log(2.0) - 3.6888794 * jax.random.uniform(seeds[8], (REPLICAS * TENSORS * CAP, BS, BS), jnp.float32) ** steps_of(seeds[8], (REPLICAS * TENSORS * CAP, BS, BS), ((0, 512),), -0.2, 0.2)), 0.05, 2.0),
    }


beta_first = 0.9
beta_second = 0.999
learn_rate = 0.01
epsilon = 1e-08
bias_first = 1.0 - 0.9 ** 10
bias_second = 1.0 - 0.999 ** 10

def slot_ranks(owners):
    count = owners.shape[0]
    earlier = lax.broadcasted_iota(jnp.int32, (count, count), 1) < lax.broadcasted_iota(jnp.int32, (count, count), 0)
    same_owner = owners[:, None] == owners[None, :]
    return lax.optimization_barrier(jnp.sum((same_owner & earlier).astype(jnp.int32), axis=1)).astype(jnp.int32)

def reference(features, gate_pre, up_pre, grad_hidden, blocks, owner, weights, moment1, moment2):
    columns = FF // N_TENSOR
    grads_list = []
    place_list = []
    for tensor_index in range(N_TENSOR):
        start_col = tensor_index * columns
        gate_value = gate_pre[:, start_col:start_col + columns].astype(jnp.float32)
        cotangent = grad_hidden[:, start_col:start_col + columns].astype(jnp.float32)
        up_value = up_pre[:, start_col:start_col + columns].astype(jnp.float32)
        sigmoid_gate = jax.nn.sigmoid(gate_value)
        grad_up = (cotangent * (gate_value * sigmoid_gate)).astype(jnp.bfloat16)
        grad_gate = (cotangent * up_value * (sigmoid_gate * (1.0 + gate_value * (1.0 - sigmoid_gate)))).astype(jnp.bfloat16)
        paired = jnp.concatenate([grad_gate, grad_up], axis=1)
        listing = blocks[tensor_index * NBT:(tensor_index + 1) * NBT]
        owners = owner[tensor_index * NBT:(tensor_index + 1) * NBT]

        def one_block(block_entry):
            rows_part = lax.dynamic_slice(features, (jnp.int32(0), block_entry[1] * BS), (TOKENS, BS))
            cols_part = lax.dynamic_slice(paired, (jnp.int32(0), block_entry[0] * columns + block_entry[2] * BS), (TOKENS, BS))
            return jnp.dot(rows_part.T, cols_part, preferred_element_type=jnp.float32)
        grads_list.append(lax.map(one_block, listing))
        place_list.append(((owners * N_TENSOR + tensor_index) * CAP + slot_ranks(owners)).astype(jnp.int32))
    block_grad = jnp.concatenate(grads_list, axis=0)
    places = jnp.concatenate(place_list, axis=0)
    first_old = moment1[places]
    second_old = moment2[places]
    weight_old = weights[places]
    first_new = beta_first * first_old + (1.0 - beta_first) * block_grad
    second_new = beta_second * second_old + (1.0 - beta_second) * block_grad * block_grad
    weight_new = weight_old - learn_rate * (first_new / bias_first) / (jnp.sqrt(second_new / bias_second) + epsilon)
    return (weights.at[places].set(weight_new), moment1.at[places].set(first_new), moment2.at[places].set(second_new))
```

```python
import functools

import jax
import jax.numpy as jnp
from jax import lax
from jax.experimental import pallas as pl
from jax.experimental.pallas import tpu as pltpu
from jax.sharding import PartitionSpec as P

beta_first = 0.9
beta_second = 0.999
learn_rate = 0.01
epsilon = 1e-08
bias_first = 1.0 - 0.9**10
bias_second = 1.0 - 0.999**10

NX, NY, NZ = 4, 8, 8
BS = 128
COLS = 14
CELLS = 8
LISTED = 64
CAP = 3
MESH = pl.DeviceIdType.MESH
RING = (
    ((0, 0), (0, 1), (1, 0), (1, 1), (2, 0), (2, 1), (3, 0)),
    ((0, 1), (0, 0), (1, 1), (1, 0), (2, 1), (2, 0), (3, 1)),
)
F32, BF16 = jnp.float32, jnp.bfloat16


def kernel(
    feat, gate, up, ghid, blk, own_s, own_v,
    bg_out, cnt_out,
    feats, gate_v, up_v, ghid_v, acts, table_v, table,
    send_c, recv_c, tot,
    x_two, x_in, x_one, x_fwd, x_left, x_right, part,
    y_half, y_half_in, y_out, y_in, gath,
    feat_sem, in_sem, table_sem, zs, zr, cs, cr, xs, xr, ys, yr, gs, gr,
):
    z = lax.axis_index("tensor")
    dp = lax.axis_index("dp")
    core = lax.rem(dp, 2)
    x = lax.rem(dp // 2, NX)
    y = dp // (2 * NX)

    def at(yy, xx, cc):
        return {"dp": (yy * NX + xx) * 2 + cc}

    def shift(v, by, n):
        return lax.rem(v + (by % n), n)

    zdev = ({"tensor": shift(z, 1, NZ)}, {"tensor": shift(z, -1, NZ)})
    xdev = {k: at(y, shift(x, k, NX), core) for k in (1, -1, 2)}
    ydev = (at(shift(y, 1, NY), x, core), at(shift(y, -1, NY), x, core))
    sib = at(y, x, 1 - core)

    in_copies = [
        pltpu.make_async_copy(s, d, in_sem.at[i])
        for i, (s, d) in enumerate(((gate, gate_v), (up, up_v), (ghid, ghid_v)))
    ]
    own_cells = [
        pltpu.make_async_copy(
            feat.at[:, pl.ds(BS * j, BS)], feats.at[z * CELLS + j], feat_sem.at[j]
        )
        for j in range(CELLS)
    ]
    for c in own_cells:
        c.start()
    for c in in_copies:
        c.start()

    barrier = pltpu.get_barrier_semaphore()
    partners = (*zdev, xdev[1], xdev[-1], xdev[2], *ydev, sib)
    for dev in partners:
        pl.semaphore_signal(barrier, inc=1, device_id=dev, device_id_type=MESH)
    pl.semaphore_wait(barrier, len(partners))

    def rcopy(src, dst, ssem, rsem, dev):
        return pltpu.make_async_remote_copy(
            src_ref=src, dst_ref=dst, send_sem=ssem, recv_sem=rsem,
            device_id=dev, device_id_type=MESH,
        )

    def ring(way, k, hop):
        dist, half = RING[way][k]
        src = shift(z, -(dist + hop) if way == 0 else dist + hop, NZ)
        cells = feats.at[pl.ds(src * CELLS + half * 4, 4)]
        return rcopy(cells, cells, zs.at[way, k], zr.at[way, k], zdev[way])

    for c in own_cells:
        c.wait()
    for k in (0, 1):
        for way in (0, 1):
            ring(way, k, 0).start()

    owner_row = own_v[...] // (2 * NX)
    wide = jnp.broadcast_to(owner_row, (LISTED, LISTED))
    tall = wide.T
    lane = lax.broadcasted_iota(jnp.int32, (LISTED, LISTED), 1)
    sub = lax.broadcasted_iota(jnp.int32, (LISTED, LISTED), 0)
    rank_row = jnp.sum(
        ((tall < wide) | ((tall == wide) & (sub < lane))).astype(jnp.int32), axis=0, keepdims=True
    )
    rank_col = jnp.broadcast_to(rank_row, (LISTED, LISTED)).T
    order_row = jnp.sum(jnp.where(rank_col == lane, sub, 0), axis=0, keepdims=True)
    start_row = jnp.sum((tall < lane).astype(jnp.int32), axis=0, keepdims=True)
    table_v[...] = jnp.zeros_like(table_v)
    table_v[0:1, 0:LISTED] = order_row
    table_v[1:2, 0:LISTED] = rank_row
    table_v[2:3, 0:LISTED] = start_row
    to_smem = pltpu.make_async_copy(table_v, table, table_sem)
    to_smem.start()

    for c in in_copies:
        c.wait()

    def make_acts(c, carry):
        cols = pl.ds(pl.multiple_of(c * BS, BS), BS)
        g = gate_v[:, cols].astype(F32)
        h = ghid_v[:, cols].astype(F32)
        u = up_v[:, cols].astype(F32)
        s = jax.nn.sigmoid(g)
        d_up = (h * (g * s)).astype(BF16)
        d_gate = (h * u * (s * (1.0 + g * (1.0 - s)))).astype(BF16)
        acts[c] = d_gate.T
        acts[c + COLS] = d_up.T
        return carry

    for k in range(2, 7):
        lax.fori_loop(3 * (k - 2), min(3 * (k - 1), COLS), make_acts, 0)
        for way in (0, 1):
            ring(way, k - 2, 1).wait_recv()
            ring(way, k, 0).start()
    to_smem.wait()

    def find(k, carry):
        count, q0, q1, q2 = carry
        mine = own_s[k] == dp
        q = table[1, k]
        q0 = jnp.where(mine & (count == 0), q, q0)
        q1 = jnp.where(mine & (count == 1), q, q1)
        q2 = jnp.where(mine & (count == 2), q, q2)
        return count + mine.astype(jnp.int32), q0, q1, q2

    zero = jnp.int32(0)
    count, *mine_at = lax.fori_loop(0, LISTED, find, (zero, zero, zero, zero))
    cnt_out[0] = count

    for k in (5, 6):
        for way in (0, 1):
            ring(way, k, 1).wait_recv()
    for k in range(7):
        for way in (0, 1):
            ring(way, k, 0).wait_send()

    def product(xx, cc, i):
        k = table[0, i * 8 + xx * 2 + cc]
        a = acts[blk[0, k] * COLS + blk[2, k]]
        return jnp.dot(a, feats[blk[1, k]], preferred_element_type=F32)

    def products(dst, n, xx, cc):
        def some(i4, carry):
            for i in range(4):
                dst[n, i4 * 4 + i] = product(xx, cc, i4 * 4 + i)
            return carry

        lax.fori_loop(0, 2, some, 0)

    rel = (2, 1, 3, 0)
    to_sib = []
    for n in range(4):
        products(send_c, n, shift(x, rel[n], NX), 1 - core)
        c = rcopy(send_c.at[n], recv_c.at[n], cs.at[n], cr.at[n], sib)
        c.start()
        to_sib.append(c)

    lo, hi = pl.ds(0, 4), pl.ds(4, 4)
    two_plus = rcopy(x_two.at[lo], x_in.at[0], xs.at[0], xr.at[0], xdev[1])
    two_minus = rcopy(x_two.at[hi], x_in.at[1], xs.at[1], xr.at[1], xdev[-1])
    one_plus = rcopy(x_one.at[0], x_left.at[hi], xs.at[2], xr.at[2], xdev[1])
    one_minus = rcopy(x_one.at[1], x_right.at[lo], xs.at[3], xr.at[3], xdev[-1])
    fwd_plus = rcopy(x_fwd.at[0], x_left.at[lo], xs.at[4], xr.at[4], xdev[1])
    fwd_minus = rcopy(x_fwd.at[1], x_right.at[hi], xs.at[5], xr.at[5], xdev[-1])
    for n in range(4):
        products(tot, n, shift(x, rel[n], NX), core)
        to_sib[n].wait_recv()
        tot[n] = tot[n] + recv_c[n]
        if n == 0:
            x_two[...] = tot[0].astype(BF16)
            two_plus.start()
            two_minus.start()
        if n == 1:
            x_one[0] = tot[1, 4:8].astype(BF16)
            one_plus.start()
        if n == 2:
            x_one[1] = tot[2, 0:4].astype(BF16)
            one_minus.start()
    two_plus.wait_recv()
    x_fwd[0] = (tot[1, 0:4] + x_in[0].astype(F32)).astype(BF16)
    fwd_plus.start()
    two_minus.wait_recv()
    x_fwd[1] = (tot[2, 4:8] + x_in[1].astype(F32)).astype(BF16)
    fwd_minus.start()
    for c in (one_plus, one_minus, fwd_plus, fwd_minus):
        c.wait_recv()
    part[...] = tot[3] + x_left[...].astype(F32) + x_right[...].astype(F32)

    col = x * 2 + core

    def first_of(yy, column):
        return (table[2, yy] + (7 - column)) // 8

    def term(yy, e):
        return part[jnp.minimum(first_of(yy, col) + e, 7)]

    rows = (slice(0, 64), slice(64, 128))
    half_copy = [
        rcopy(y_half.at[w], y_half_in.at[w], ys.at[w, 0], yr.at[w, 0], ydev[w]) for w in (0, 1)
    ]
    y_copy = [
        [
            rcopy(y_out.at[w, t], y_in.at[w, t], ys.at[w, t + 1], yr.at[w, t + 1], ydev[w])
            for t in range(3)
        ]
        for w in (0, 1)
    ]
    for w in (0, 1):
        for e in range(CAP):
            y_half[w, e] = term(shift(y, 4, NY), e)[rows[w]].astype(BF16)
        half_copy[w].start()
    for t in range(3):
        for w in (0, 1):
            yy = shift(y, 3 - t if w == 0 else t - 3, NY)
            if t == 0:
                half_copy[w].wait_recv()
            else:
                y_copy[w][t - 1].wait_recv()
            for e in range(CAP):
                v = term(yy, e)
                if t == 0:
                    got = y_half_in[w, e].astype(F32)
                    y_out[w, t, e, rows[w]] = (v[rows[w]] + got).astype(BF16)
                    y_out[w, t, e, rows[1 - w]] = v[rows[1 - w]].astype(BF16)
                else:
                    y_out[w, t, e] = (v + y_in[w, t - 1, e].astype(F32)).astype(BF16)
            y_copy[w][t].start()
    for w in (0, 1):
        y_copy[w][2].wait_recv()
    for e in range(CAP):
        gath[col * CAP + e] = (
            term(y, e) + y_in[0, 2, e].astype(F32) + y_in[1, 2, e].astype(F32)
        )

    def column(cc):
        return gath.at[pl.ds(cc * CAP, CAP)]

    x_copy = []
    for n, k in enumerate((2, 1, -1)):
        c = rcopy(column(col), column(col), gs.at[n], gr.at[n], xdev[k])
        c.start()
        x_copy.append(c)
    sib_copy = [rcopy(column(col), column(col), gs.at[3], gr.at[3], sib)]
    sib_copy[0].start()
    for n, k in ((1, 1), (2, -1), (0, 2)):
        x_copy[n].wait_recv()
        came = column(shift(x, -k, NX) * 2 + core)
        c = rcopy(came, came, gs.at[4 + n], gr.at[4 + n], sib)
        c.start()
        sib_copy.append(c)
    for c in sib_copy:
        c.wait_recv()
    for s in range(CAP):
        q = mine_at[s]
        column_of = lax.rem(q, 8)
        e = q // 8 - first_of(y, column_of)
        at_row = jnp.clip(column_of * CAP + e, 0, 8 * CAP - 1)
        bg_out[s] = gath[at_row].T

    for c in (*to_sib, two_plus, two_minus, one_plus, one_minus, fwd_plus, fwd_minus,
              *half_copy, *y_copy[0], *y_copy[1], *x_copy, *sib_copy):
        c.wait_send()


def local(features, gate_pre, up_pre, grad_hidden, blocks, owner, weights, moment1, moment2):
    any_ = pl.BlockSpec(memory_space=pl.ANY)
    smem = pl.BlockSpec(memory_space=pltpu.SMEM)
    vmem = pl.BlockSpec(memory_space=pltpu.VMEM)
    tokens = features.shape[0]
    dma = pltpu.SemaphoreType.DMA
    block_grad, count = pl.pallas_call(
        kernel,
        out_shape=(
            jax.ShapeDtypeStruct((CAP, BS, BS), F32),
            jax.ShapeDtypeStruct((1,), jnp.int32),
        ),
        in_specs=[any_, any_, any_, any_, smem, smem, vmem],
        out_specs=(vmem, smem),
        scratch_shapes=[
            pltpu.VMEM((NZ * CELLS, tokens, BS), BF16),
            pltpu.VMEM(gate_pre.shape, BF16),
            pltpu.VMEM(gate_pre.shape, BF16),
            pltpu.VMEM(gate_pre.shape, BF16),
            pltpu.VMEM((2 * COLS, BS, tokens), BF16),
            pltpu.VMEM((8, 128), jnp.int32),
            pltpu.SMEM((8, 128), jnp.int32),
            pltpu.VMEM((4, 8, BS, BS), F32),
            pltpu.VMEM((4, 8, BS, BS), F32),
            pltpu.VMEM((4, 8, BS, BS), F32),
            pltpu.VMEM((8, BS, BS), BF16),
            pltpu.VMEM((2, 4, BS, BS), BF16),
            pltpu.VMEM((2, 4, BS, BS), BF16),
            pltpu.VMEM((2, 4, BS, BS), BF16),
            pltpu.VMEM((8, BS, BS), BF16),
            pltpu.VMEM((8, BS, BS), BF16),
            pltpu.VMEM((8, BS, BS), F32),
            pltpu.VMEM((2, CAP, BS // 2, BS), BF16),
            pltpu.VMEM((2, CAP, BS // 2, BS), BF16),
            pltpu.VMEM((2, 3, CAP, BS, BS), BF16),
            pltpu.VMEM((2, 3, CAP, BS, BS), BF16),
            pltpu.VMEM((8 * CAP, BS, BS), F32),
            dma((CELLS,)),
            dma((3,)),
            dma,
            dma((2, 7)),
            dma((2, 7)),
            dma((4,)),
            dma((4,)),
            dma((6,)),
            dma((6,)),
            dma((2, 4)),
            dma((2, 4)),
            dma((7,)),
            dma((7,)),
        ],
        compiler_params=pltpu.CompilerParams(
            collective_id=0, has_side_effects=True, vmem_limit_bytes=48 * 2**20
        ),
        cost_estimate=pl.CostEstimate(
            flops=2 * LISTED * tokens * BS * BS, bytes_accessed=4 * 2**20, transcendentals=tokens * COLS * BS
        ),
        name="block_grads",
    )(features, gate_pre, up_pre, grad_hidden, blocks.T, owner, owner.reshape(1, LISTED))
    is_valid = (jnp.arange(CAP, dtype=jnp.int32) < count[0])[:, None, None]
    first_new = beta_first * moment1 + (1.0 - beta_first) * block_grad
    second_new = beta_second * moment2 + (1.0 - beta_second) * block_grad * block_grad
    weight_new = weights - learn_rate * (first_new / bias_first) / (
        jnp.sqrt(second_new / bias_second) + epsilon
    )
    return (
        jnp.where(is_valid, weight_new, weights),
        jnp.where(is_valid, first_new, moment1),
        jnp.where(is_valid, second_new, moment2),
    )


def solution(mesh):
    tokens = P("dp", "tensor")
    state = P(("dp", "tensor"), None, None)
    return jax.shard_map(
        local,
        mesh=mesh,
        in_specs=(tokens,) * 4 + (P("tensor", None), P("tensor")) + (state,) * 3,
        out_specs=(state,) * 3,
        check_vma=False,
    )
```

```python
import functools

import jax
import jax.numpy as jnp
from jax import lax
from jax.experimental import pallas as pl
from jax.experimental.pallas import tpu as pltpu
from jax.sharding import PartitionSpec as P

beta_first = 0.9
beta_second = 0.999
learn_rate = 0.01
epsilon = 1e-08
bias_first = 1.0 - 0.9**10
bias_second = 1.0 - 0.999**10

NX, NY, NZ = 4, 8, 8
BS = 128
COLS = 14
CELLS = 8
LISTED = 64
CAP = 3
MESH = pl.DeviceIdType.MESH
PARTS = 4
ROWS = BS // PARTS
LAG = 0
CHUNK = 4
PER = CELLS // CHUNK
RING = tuple(
    [(d, c) for d in range(3) for c in order] + [(3, c) for c in order[: PER // 2]]
    for order in (list(range(PER)), list(range(PER))[::-1])
)
HOPS = len(RING[0])
F32, BF16 = jnp.float32, jnp.bfloat16


def kernel(
    feat, gate, up, ghid, blk, own_s, own_v,
    bg_out, cnt_out,
    feats, gate_v, up_v, ghid_v, acts, table_v, table,
    send_c, recv_c, tot,
    x_two, x_in, x_one, x_fwd, x_left, x_right, part,
    y_out, y_in, gath,
    feat_sem, in_sem, table_sem, zs, zr, cs, cr, xs, xr, ys, yr, gs, gr,
):
    z = lax.axis_index("tensor")
    dp = lax.axis_index("dp")
    core = lax.rem(dp, 2)
    x = lax.rem(dp // 2, NX)
    y = dp // (2 * NX)

    def at(yy, xx, cc):
        return {"dp": (yy * NX + xx) * 2 + cc}

    def shift(v, by, n):
        return lax.rem(v + (by % n), n)

    zdev = ({"tensor": shift(z, 1, NZ)}, {"tensor": shift(z, -1, NZ)})
    xdev = {k: at(y, shift(x, k, NX), core) for k in (1, -1, 2)}
    ydev = {k: at(shift(y, k, NY), x, core) for k in (1, -1, 2, -2)}
    sib = at(y, x, 1 - core)

    in_copies = [
        pltpu.make_async_copy(s, d, in_sem.at[i])
        for i, (s, d) in enumerate(((gate, gate_v), (up, up_v), (ghid, ghid_v)))
    ]
    own_cells = [
        pltpu.make_async_copy(
            feat.at[:, pl.ds(BS * j, BS)], feats.at[z * CELLS + j], feat_sem.at[j]
        )
        for j in range(CELLS)
    ]
    for c in own_cells:
        c.start()
    for c in in_copies:
        c.start()

    barrier = pltpu.get_barrier_semaphore()
    partners = (*zdev, *xdev.values(), *ydev.values(), sib)
    for dev in partners:
        pl.semaphore_signal(barrier, inc=1, device_id=dev, device_id_type=MESH)
    pl.semaphore_wait(barrier, len(partners))

    def rcopy(src, dst, ssem, rsem, dev):
        return pltpu.make_async_remote_copy(
            src_ref=src, dst_ref=dst, send_sem=ssem, recv_sem=rsem,
            device_id=dev, device_id_type=MESH,
        )

    def ring(way, k, hop):
        dist, half = RING[way][k]
        src = shift(z, -(dist + hop) if way == 0 else dist + hop, NZ)
        cells = feats.at[pl.ds(src * CELLS + half * CHUNK, CHUNK)]
        return rcopy(cells, cells, zs.at[way, k], zr.at[way, k], zdev[way])

    for c in own_cells:
        c.wait()
    for k in range(PER):
        for way in (0, 1):
            ring(way, k, 0).start()

    owner_row = own_v[...] // (2 * NX)
    wide = jnp.broadcast_to(owner_row, (LISTED, LISTED))
    tall = wide.T
    lane = lax.broadcasted_iota(jnp.int32, (LISTED, LISTED), 1)
    sub = lax.broadcasted_iota(jnp.int32, (LISTED, LISTED), 0)
    rank_row = jnp.sum(
        ((tall < wide) | ((tall == wide) & (sub < lane))).astype(jnp.int32), axis=0, keepdims=True
    )
    rank_col = jnp.broadcast_to(rank_row, (LISTED, LISTED)).T
    order_row = jnp.sum(jnp.where(rank_col == lane, sub, 0), axis=0, keepdims=True)
    start_row = jnp.sum((tall < lane).astype(jnp.int32), axis=0, keepdims=True)
    table_v[...] = jnp.zeros_like(table_v)
    table_v[0:1, 0:LISTED] = order_row
    table_v[1:2, 0:LISTED] = rank_row
    table_v[2:3, 0:LISTED] = start_row
    to_smem = pltpu.make_async_copy(table_v, table, table_sem)
    to_smem.start()

    for c in in_copies:
        c.wait()

    def make_acts(c, carry):
        cols = pl.ds(pl.multiple_of(c * BS, BS), BS)
        g = gate_v[:, cols].astype(F32)
        h = ghid_v[:, cols].astype(F32)
        u = up_v[:, cols].astype(F32)
        s = jax.nn.sigmoid(g)
        d_up = (h * (g * s)).astype(BF16)
        d_gate = (h * u * (s * (1.0 + g * (1.0 - s)))).astype(BF16)
        acts[c] = d_gate.T
        acts[c + COLS] = d_up.T
        return carry

    done = 0
    for k in range(PER, HOPS):
        upto = min(COLS, (k - PER + 1) * COLS // (HOPS - PER - 1))
        if upto > done:
            lax.fori_loop(done, upto, make_acts, 0)
            done = upto
        for way in (0, 1):
            ring(way, k - PER, 1).wait_recv()
            ring(way, k, 0).start()
    to_smem.wait()

    def find(k, carry):
        count, q0, q1, q2 = carry
        mine = own_s[k] == dp
        q = table[1, k]
        q0 = jnp.where(mine & (count == 0), q, q0)
        q1 = jnp.where(mine & (count == 1), q, q1)
        q2 = jnp.where(mine & (count == 2), q, q2)
        return count + mine.astype(jnp.int32), q0, q1, q2

    zero = jnp.int32(0)
    count, *mine_at = lax.fori_loop(0, LISTED, find, (zero, zero, zero, zero))
    cnt_out[0] = count

    for k in range(HOPS - PER, HOPS):
        for way in (0, 1):
            ring(way, k, 1).wait_recv()
    for k in range(HOPS):
        for way in (0, 1):
            ring(way, k, 0).wait_send()

    def product(xx, cc, i):
        k = table[0, i * 8 + xx * 2 + cc]
        a = acts[blk[0, k] * COLS + blk[2, k]]
        return jnp.dot(a, feats[blk[1, k]], preferred_element_type=F32)

    def products(dst, n, xx, cc):
        for i in range(8):
            dst[n, i] = product(xx, cc, i)

    rel = (2, 1, 3, 0)
    sent = []

    def send(*copy):
        c = rcopy(*copy)
        c.start()
        sent.append(c)
        return c

    to_sib = {}

    def for_sib(n):
        products(send_c, n, shift(x, rel[n], NX), 1 - core)
        to_sib[n] = send(send_c.at[n], recv_c.at[n], cs.at[n], cr.at[n], sib)

    def for_me(n):
        products(tot, n, shift(x, rel[n], NX), core)

    def rows_of(h):
        return pl.ds(h * ROWS, ROWS)

    lo, hi = pl.ds(0, 4), pl.ds(4, 4)
    along_x = [{} for _ in range(PARTS)]

    def to_x(h, name, n, src, dst, step):
        along_x[h][name] = send(src, dst, xs.at[h, n], xr.at[h, n], xdev[step])

    def core_sum(n):
        to_sib[n].wait_recv()
        tot[n] = tot[n] + recv_c[n]
        for h in range(PARTS if n == 0 else 0):
            if n == 0:
                x_two[h] = tot[0, :, rows_of(h)].astype(BF16)
                to_x(h, "two+", 0, x_two.at[h, lo], x_in.at[h, 0], 1)
                to_x(h, "two-", 1, x_two.at[h, hi], x_in.at[h, 1], -1)

    for_sib(0)
    for_sib(1)
    for_me(0)
    core_sum(0)
    for_me(1)
    for_sib(2)
    core_sum(1)
    for_me(2)
    for_sib(3)
    core_sum(2)
    for_me(3)
    core_sum(3)

    col = x * 2 + core

    def first_of(yy, column):
        return (table[2, yy] + (7 - column)) // 8

    def column(cc, h):
        return gath.at[pl.ds(cc * CAP, CAP), rows_of(h)]

    def tail(h):
        mine = rows_of(h)
        moves = along_x[h]
        x_one[h, 0] = tot[1, hi, mine].astype(BF16)
        to_x(h, "one+", 2, x_one.at[h, 0], x_left.at[h, hi], 1)
        x_one[h, 1] = tot[2, lo, mine].astype(BF16)
        to_x(h, "one-", 3, x_one.at[h, 1], x_right.at[h, lo], -1)
        moves["two+"].wait_recv()
        x_fwd[h, 0] = (tot[1, lo, mine] + x_in[h, 0].astype(F32)).astype(BF16)
        to_x(h, "fwd+", 4, x_fwd.at[h, 0], x_left.at[h, lo], 1)
        moves["two-"].wait_recv()
        x_fwd[h, 1] = (tot[2, hi, mine] + x_in[h, 1].astype(F32)).astype(BF16)
        to_x(h, "fwd-", 5, x_fwd.at[h, 1], x_right.at[h, hi], -1)
        yield
        for name in ("one+", "one-", "fwd+", "fwd-"):
            moves[name].wait_recv()
        part[:, mine] = tot[3, :, mine] + x_left[h].astype(F32) + x_right[h].astype(F32)

        def term(yy, e):
            return part[jnp.minimum(first_of(yy, col) + e, 7), mine]

        def along_y(way, kind, dist, hop, came=()):
            sign = 1 if way == 0 else -1
            yy = shift(y, sign * dist, NY)
            for e in range(CAP):
                v = term(yy, e)
                for k in came:
                    v = v + y_in[h, way, k, e].astype(F32)
                y_out[h, way, kind, e] = v.astype(BF16)
            return send(
                y_out.at[h, way, kind], y_in.at[h, way, kind],
                ys.at[h, way, kind], yr.at[h, way, kind], ydev[sign * hop],
            )

        far = h % 2
        ways = (far, 1 - far)
        third = {w: along_y(w, 0, 3, 1) for w in ways}
        fourth = along_y(far, 2, 4, 2)
        first = {w: along_y(w, 1, 1, 1) for w in ways}
        yield
        second = {}
        for w in ways:
            third[w].wait_recv()
            if w == far:
                fourth.wait_recv()
            second[w] = along_y(w, 3, 2, 2, (0, 2) if w == far else (0,))
        yield
        for w in ways:
            first[w].wait_recv()
            second[w].wait_recv()
        for e in range(CAP):
            v = term(y, e)
            for w in (0, 1):
                v = v + (y_in[h, w, 1, e].astype(F32) + y_in[h, w, 3, e].astype(F32))
            gath[col * CAP + e, mine] = v

        own = column(col, h)
        x_copy = [send(own, own, gs.at[h, n], gr.at[h, n], xdev[k]) for n, k in enumerate((2, 1, -1))]
        sib_copy = [send(own, own, gs.at[h, 3], gr.at[h, 3], sib)]
        yield
        for n, k in ((1, 1), (2, -1), (0, 2)):
            x_copy[n].wait_recv()
            came = column(shift(x, -k, NX) * 2 + core, h)
            sib_copy.append(send(came, came, gs.at[h, 4 + n], gr.at[h, 4 + n], sib))
        yield
        for c in sib_copy:
            c.wait_recv()

    turns = [tail(h) for h in range(PARTS)]
    for turn in turns:
        next(turn)
    running, slot = set(range(PARTS)), 0
    while running:
        for h in sorted(running):
            if h * LAG <= slot and next(turns[h], turns) is turns:
                running.remove(h)
        slot += 1

    for s in range(CAP):
        q = mine_at[s]
        column_of = lax.rem(q, 8)
        e = q // 8 - first_of(y, column_of)
        at_row = jnp.clip(column_of * CAP + e, 0, 8 * CAP - 1)
        bg_out[s] = gath[at_row].T

    for c in sent:
        c.wait_send()


def local(features, gate_pre, up_pre, grad_hidden, blocks, owner, weights, moment1, moment2):
    hbm = pl.BlockSpec(memory_space=pltpu.HBM)
    smem = pl.BlockSpec(memory_space=pltpu.SMEM)
    vmem = pl.BlockSpec(memory_space=pltpu.VMEM)
    tokens = features.shape[0]
    dma = pltpu.SemaphoreType.DMA
    block_grad, count = pl.pallas_call(
        kernel,
        out_shape=(
            jax.ShapeDtypeStruct((CAP, BS, BS), F32),
            jax.ShapeDtypeStruct((1,), jnp.int32),
        ),
        in_specs=[hbm, hbm, hbm, hbm, smem, smem, vmem],
        out_specs=(vmem, smem),
        scratch_shapes=[
            pltpu.VMEM((NZ * CELLS, tokens, BS), BF16),
            pltpu.VMEM(gate_pre.shape, BF16),
            pltpu.VMEM(gate_pre.shape, BF16),
            pltpu.VMEM(gate_pre.shape, BF16),
            pltpu.VMEM((2 * COLS, BS, tokens), BF16),
            pltpu.VMEM((8, 128), jnp.int32),
            pltpu.SMEM((8, 128), jnp.int32),
            pltpu.VMEM((4, 8, BS, BS), F32),
            pltpu.VMEM((4, 8, BS, BS), F32),
            pltpu.VMEM((4, 8, BS, BS), F32),
            pltpu.VMEM((PARTS, 8, ROWS, BS), BF16),
            pltpu.VMEM((PARTS, 2, 4, ROWS, BS), BF16),
            pltpu.VMEM((PARTS, 2, 4, ROWS, BS), BF16),
            pltpu.VMEM((PARTS, 2, 4, ROWS, BS), BF16),
            pltpu.VMEM((PARTS, 8, ROWS, BS), BF16),
            pltpu.VMEM((PARTS, 8, ROWS, BS), BF16),
            pltpu.VMEM((8, BS, BS), F32),
            pltpu.VMEM((PARTS, 2, 4, CAP, ROWS, BS), BF16),
            pltpu.VMEM((PARTS, 2, 4, CAP, ROWS, BS), BF16),
            pltpu.VMEM((8 * CAP, BS, BS), F32),
            dma((CELLS,)),
            dma((3,)),
            dma,
            dma((2, HOPS)),
            dma((2, HOPS)),
            dma((4,)),
            dma((4,)),
            dma((PARTS, 6)),
            dma((PARTS, 6)),
            dma((PARTS, 2, 4)),
            dma((PARTS, 2, 4)),
            dma((PARTS, 7)),
            dma((PARTS, 7)),
        ],
        compiler_params=pltpu.CompilerParams(
            collective_id=0, has_side_effects=True, vmem_limit_bytes=60 * 2**20
        ),
        cost_estimate=pl.CostEstimate(
            flops=2 * LISTED * tokens * BS * BS, bytes_accessed=4 * 2**20, transcendentals=tokens * COLS * BS
        ),
        name="block_grads",
    )(features, gate_pre, up_pre, grad_hidden, blocks.T, owner, owner.reshape(1, LISTED))
    is_valid = (jnp.arange(CAP, dtype=jnp.int32) < count[0])[:, None, None]
    first_new = beta_first * moment1 + (1.0 - beta_first) * block_grad
    second_new = beta_second * moment2 + (1.0 - beta_second) * block_grad * block_grad
    weight_new = weights - learn_rate * (first_new / bias_first) / (
        jnp.sqrt(second_new / bias_second) + epsilon
    )
    return (
        jnp.where(is_valid, weight_new, weights),
        jnp.where(is_valid, first_new, moment1),
        jnp.where(is_valid, second_new, moment2),
    )


def solution(mesh):
    tokens = P("dp", "tensor")
    state = P(("dp", "tensor"), None, None)
    return jax.shard_map(
        local,
        mesh=mesh,
        in_specs=(tokens,) * 4 + (P("tensor", None), P("tensor")) + (state,) * 3,
        out_specs=(state,) * 3,
        check_vma=False,
    )
```

```python
import functools

import jax
import jax.numpy as jnp
from jax import lax
from jax.experimental import pallas as pl
from jax.experimental.pallas import tpu as pltpu
from jax.sharding import PartitionSpec as P

beta_first = 0.9
beta_second = 0.999
learn_rate = 0.01
epsilon = 1e-08
bias_first = 1.0 - 0.9**10
bias_second = 1.0 - 0.999**10

NX, NY, NZ = 4, 8, 8
BS = 128
COLS = 14
CELLS = 8
LISTED = 64
CAP = 3
MESH = pl.DeviceIdType.MESH
PARTS = 4
ROWS = BS // PARTS
ORDER = (0, 1, 2, 0, 3, 1, 2, 0, 3, 1, 2, 0, 3, 1, 2, 0, 3, 1, 2, 3)
CHUNK = 4
PER = CELLS // CHUNK
RING = tuple(
    [(d, c) for d in range(3) for c in order] + [(3, c) for c in order[: PER // 2]]
    for order in (list(range(PER)), list(range(PER))[::-1])
)
HOPS = len(RING[0])
F32, BF16 = jnp.float32, jnp.bfloat16


def kernel(
    feat, gate, up, ghid, blk, own_s, own_v,
    bg_out, cnt_out,
    feats, gate_v, up_v, ghid_v, acts, table_v, table,
    send_c, recv_c, tot,
    x_two, x_in, x_one, x_fwd, x_left, x_right, part,
    y_out, y_in, gath,
    feat_sem, in_sem, table_sem, zs, zr, cs, cr, xs, xr, ys, yr, gs, gr,
):
    z = lax.axis_index("tensor")
    dp = lax.axis_index("dp")
    core = lax.rem(dp, 2)
    x = lax.rem(dp // 2, NX)
    y = dp // (2 * NX)

    def at(yy, xx, cc):
        return {"dp": (yy * NX + xx) * 2 + cc}

    def shift(v, by, n):
        return lax.rem(v + (by % n), n)

    zdev = ({"tensor": shift(z, 1, NZ)}, {"tensor": shift(z, -1, NZ)})
    xdev = {k: at(y, shift(x, k, NX), core) for k in (1, -1, 2)}
    ydev = {k: at(shift(y, k, NY), x, core) for k in (1, -1, 2, -2)}
    sib = at(y, x, 1 - core)

    in_copies = [
        pltpu.make_async_copy(s, d, in_sem.at[i])
        for i, (s, d) in enumerate(((gate, gate_v), (up, up_v), (ghid, ghid_v)))
    ]
    own_cells = [
        pltpu.make_async_copy(
            feat.at[:, pl.ds(BS * j, BS)], feats.at[z * CELLS + j], feat_sem.at[j]
        )
        for j in range(CELLS)
    ]
    for c in own_cells:
        c.start()
    for c in in_copies:
        c.start()

    barrier = pltpu.get_barrier_semaphore()
    partners = (*zdev, *xdev.values(), *ydev.values(), sib)
    for dev in partners:
        pl.semaphore_signal(barrier, inc=1, device_id=dev, device_id_type=MESH)
    pl.semaphore_wait(barrier, len(partners))

    def rcopy(src, dst, ssem, rsem, dev):
        return pltpu.make_async_remote_copy(
            src_ref=src, dst_ref=dst, send_sem=ssem, recv_sem=rsem,
            device_id=dev, device_id_type=MESH,
        )

    def ring(way, k, hop):
        dist, half = RING[way][k]
        src = shift(z, -(dist + hop) if way == 0 else dist + hop, NZ)
        cells = feats.at[pl.ds(src * CELLS + half * CHUNK, CHUNK)]
        return rcopy(cells, cells, zs.at[way, k], zr.at[way, k], zdev[way])

    for c in own_cells:
        c.wait()
    for k in range(PER):
        for way in (0, 1):
            ring(way, k, 0).start()

    owner_row = own_v[...] // (2 * NX)
    wide = jnp.broadcast_to(owner_row, (LISTED, LISTED))
    tall = wide.T
    lane = lax.broadcasted_iota(jnp.int32, (LISTED, LISTED), 1)
    sub = lax.broadcasted_iota(jnp.int32, (LISTED, LISTED), 0)
    rank_row = jnp.sum(
        ((tall < wide) | ((tall == wide) & (sub < lane))).astype(jnp.int32), axis=0, keepdims=True
    )
    rank_col = jnp.broadcast_to(rank_row, (LISTED, LISTED)).T
    order_row = jnp.sum(jnp.where(rank_col == lane, sub, 0), axis=0, keepdims=True)
    start_row = jnp.sum((tall < lane).astype(jnp.int32), axis=0, keepdims=True)
    table_v[...] = jnp.zeros_like(table_v)
    table_v[0:1, 0:LISTED] = order_row
    table_v[1:2, 0:LISTED] = rank_row
    table_v[2:3, 0:LISTED] = start_row
    to_smem = pltpu.make_async_copy(table_v, table, table_sem)
    to_smem.start()

    for c in in_copies:
        c.wait()

    def make_acts(c, carry):
        cols = pl.ds(pl.multiple_of(c * BS, BS), BS)
        g = gate_v[:, cols].astype(F32)
        h = ghid_v[:, cols].astype(F32)
        u = up_v[:, cols].astype(F32)
        s = jax.nn.sigmoid(g)
        d_up = (h * (g * s)).astype(BF16)
        d_gate = (h * u * (s * (1.0 + g * (1.0 - s)))).astype(BF16)
        acts[c] = d_gate.T
        acts[c + COLS] = d_up.T
        return carry

    done = 0
    for k in range(PER, HOPS):
        upto = min(COLS, (k - PER + 1) * COLS // (HOPS - PER - 1))
        if upto > done:
            lax.fori_loop(done, upto, make_acts, 0)
            done = upto
        for way in (0, 1):
            ring(way, k - PER, 1).wait_recv()
            ring(way, k, 0).start()
    to_smem.wait()

    def find(k, carry):
        count, q0, q1, q2 = carry
        mine = own_s[k] == dp
        q = table[1, k]
        q0 = jnp.where(mine & (count == 0), q, q0)
        q1 = jnp.where(mine & (count == 1), q, q1)
        q2 = jnp.where(mine & (count == 2), q, q2)
        return count + mine.astype(jnp.int32), q0, q1, q2

    zero = jnp.int32(0)
    count, *mine_at = lax.fori_loop(0, LISTED, find, (zero, zero, zero, zero))
    cnt_out[0] = count

    for k in range(HOPS - PER, HOPS):
        for way in (0, 1):
            ring(way, k, 1).wait_recv()

    def product(xx, cc, i):
        k = table[0, i * 8 + xx * 2 + cc]
        a = acts[blk[0, k] * COLS + blk[2, k]]
        return jnp.dot(a, feats[blk[1, k]], preferred_element_type=F32)

    def products(dst, n, xx, cc, places=range(8)):
        for i in places:
            dst[n, i] = product(xx, cc, i)

    rel = (2, 1, 3, 0)
    sent = []

    def send(*copy):
        c = rcopy(*copy)
        c.start()
        return c

    to_sib = {}

    def for_sib(n):
        xx = shift(x, rel[n], NX)
        for m in (0, 1) if n == 0 else (0,):
            places = slice(4 * m, 4 * m + 4) if n == 0 else slice(0, 8)
            products(send_c, n, xx, 1 - core, range(8)[places])
            part_c = pl.ds(places.start, places.stop - places.start)
            to_sib[n, m] = send(
                send_c.at[n, part_c], recv_c.at[n, part_c], cs.at[n, m], cr.at[n, m], sib
            )

    def for_me(n):
        products(tot, n, shift(x, rel[n], NX), core)

    def rows_of(h):
        return pl.ds(h * ROWS, ROWS)

    lo, hi = pl.ds(0, 4), pl.ds(4, 4)
    along_x = [{} for _ in range(PARTS)]

    def to_x(h, name, n, src, dst, step):
        along_x[h][name] = send(src, dst, xs.at[h, n], xr.at[h, n], xdev[step])

    def core_sum(n):
        if n > 0:
            to_sib[n, 0].wait_recv()
            tot[n] = tot[n] + recv_c[n]
            return
        for m, (places, step) in enumerate(((lo, 1), (hi, -1))):
            to_sib[0, m].wait_recv()
            for h in range(PARTS):
                x_two[h, places] = (tot[0, places, rows_of(h)] + recv_c[0, places, rows_of(h)]).astype(BF16)
                to_x(h, ("two+", "two-")[m], m, x_two.at[h, places], x_in.at[h, m], step)

    for_sib(0)
    for_sib(1)
    for_me(0)
    core_sum(0)
    for_sib(2)
    for_me(1)
    core_sum(1)
    for_me(2)
    core_sum(2)

    col = x * 2 + core

    def first_of(yy, column):
        return (table[2, yy] + (7 - column)) // 8

    def column(cc, h):
        return gath.at[pl.ds(cc * CAP, CAP), rows_of(h)]

    def tail(h):
        mine = rows_of(h)
        moves = along_x[h]
        x_one[h, 0] = tot[1, hi, mine].astype(BF16)
        to_x(h, "one+", 2, x_one.at[h, 0], x_left.at[h, hi], 1)
        x_one[h, 1] = tot[2, lo, mine].astype(BF16)
        to_x(h, "one-", 3, x_one.at[h, 1], x_right.at[h, lo], -1)
        yield
        moves["two+"].wait_recv()
        x_fwd[h, 0] = (tot[1, lo, mine] + x_in[h, 0].astype(F32)).astype(BF16)
        to_x(h, "fwd+", 4, x_fwd.at[h, 0], x_left.at[h, lo], 1)
        moves["two-"].wait_recv()
        x_fwd[h, 1] = (tot[2, hi, mine] + x_in[h, 1].astype(F32)).astype(BF16)
        to_x(h, "fwd-", 5, x_fwd.at[h, 1], x_right.at[h, hi], -1)
        yield
        for name in ("one+", "one-", "fwd+", "fwd-"):
            moves[name].wait_recv()
        part[:, mine] = tot[3, :, mine] + x_left[h].astype(F32) + x_right[h].astype(F32)

        def term(yy, e):
            return part[jnp.minimum(first_of(yy, col) + e, 7), mine]

        def along_y(way, kind, dist, hop, came=()):
            sign = 1 if way == 0 else -1
            yy = shift(y, sign * dist, NY)
            for e in range(CAP):
                v = term(yy, e)
                for k in came:
                    v = v + y_in[h, way, k, e].astype(F32)
                y_out[h, way, kind, e] = v.astype(BF16)
            return send(
                y_out.at[h, way, kind], y_in.at[h, way, kind],
                ys.at[h, way, kind], yr.at[h, way, kind], ydev[sign * hop],
            )

        far = h % 2
        ways = (far, 1 - far)
        third = {w: along_y(w, 0, 3, 1) for w in ways}
        fourth = along_y(far, 2, 4, 2)
        yield
        if h == 0:
            for k in range(HOPS):
                for way in (0, 1):
                    ring(way, k, 0).wait_send()
            for c in to_sib.values():
                c.wait_send()
        first, second = {}, {}
        for w in ways:
            third[w].wait_recv()
            if w == far:
                fourth.wait_recv()
            second[w] = along_y(w, 3, 2, 2, (0, 2) if w == far else (0,))
        for w in ways:
            first[w] = along_y(w, 1, 1, 1)
        yield
        for c in moves.values():
            c.wait_send()
        for w in ways:
            first[w].wait_recv()
            second[w].wait_recv()
        for e in range(CAP):
            v = term(y, e)
            for w in (0, 1):
                v = v + (y_in[h, w, 1, e].astype(F32) + y_in[h, w, 3, e].astype(F32))
            gath[col * CAP + e, mine] = v

        own = column(col, h)
        x_copy = [send(own, own, gs.at[h, n], gr.at[h, n], xdev[k]) for n, k in enumerate((2, 1, -1))]
        sib_copy = [send(own, own, gs.at[h, 3], gr.at[h, 3], sib)]
        yield
        for n, k in ((1, 1), (2, -1), (0, 2)):
            x_copy[n].wait_recv()
            came = column(shift(x, -k, NX) * 2 + core, h)
            sib_copy.append(send(came, came, gs.at[h, 4 + n], gr.at[h, 4 + n], sib))
        for c in (*third.values(), fourth, *first.values(), *second.values()):
            c.wait_send()
        yield
        for c in sib_copy:
            c.wait_recv()
        sent.extend((*x_copy, *sib_copy))

    turns = [tail(h) for h in range(PARTS)]
    next(turns[0])
    for_sib(3)
    for_me(3)
    next(turns[0])
    for turn in turns[1:]:
        next(turn)
        next(turn)
    core_sum(3)
    for h in ORDER:
        next(turns[h], None)

    for s in range(CAP):
        q = mine_at[s]
        column_of = lax.rem(q, 8)
        e = q // 8 - first_of(y, column_of)
        at_row = jnp.clip(column_of * CAP + e, 0, 8 * CAP - 1)
        bg_out[s] = gath[at_row].T

    for c in sent:
        c.wait_send()


def local(features, gate_pre, up_pre, grad_hidden, blocks, owner, weights, moment1, moment2):
    hbm = pl.BlockSpec(memory_space=pltpu.HBM)
    smem = pl.BlockSpec(memory_space=pltpu.SMEM)
    vmem = pl.BlockSpec(memory_space=pltpu.VMEM)
    tokens = features.shape[0]
    dma = pltpu.SemaphoreType.DMA
    block_grad, count = pl.pallas_call(
        kernel,
        out_shape=(
            jax.ShapeDtypeStruct((CAP, BS, BS), F32),
            jax.ShapeDtypeStruct((1,), jnp.int32),
        ),
        in_specs=[hbm, hbm, hbm, hbm, smem, smem, vmem],
        out_specs=(vmem, smem),
        scratch_shapes=[
            pltpu.VMEM((NZ * CELLS, tokens, BS), BF16),
            pltpu.VMEM(gate_pre.shape, BF16),
            pltpu.VMEM(gate_pre.shape, BF16),
            pltpu.VMEM(gate_pre.shape, BF16),
            pltpu.VMEM((2 * COLS, BS, tokens), BF16),
            pltpu.VMEM((8, 128), jnp.int32),
            pltpu.SMEM((8, 128), jnp.int32),
            pltpu.VMEM((4, 8, BS, BS), F32),
            pltpu.VMEM((4, 8, BS, BS), F32),
            pltpu.VMEM((4, 8, BS, BS), F32),
            pltpu.VMEM((PARTS, 8, ROWS, BS), BF16),
            pltpu.VMEM((PARTS, 2, 4, ROWS, BS), BF16),
            pltpu.VMEM((PARTS, 2, 4, ROWS, BS), BF16),
            pltpu.VMEM((PARTS, 2, 4, ROWS, BS), BF16),
            pltpu.VMEM((PARTS, 8, ROWS, BS), BF16),
            pltpu.VMEM((PARTS, 8, ROWS, BS), BF16),
            pltpu.VMEM((8, BS, BS), F32),
            pltpu.VMEM((PARTS, 2, 4, CAP, ROWS, BS), BF16),
            pltpu.VMEM((PARTS, 2, 4, CAP, ROWS, BS), BF16),
            pltpu.VMEM((8 * CAP, BS, BS), F32),
            dma((CELLS,)),
            dma((3,)),
            dma,
            dma((2, HOPS)),
            dma((2, HOPS)),
            dma((4, 2)),
            dma((4, 2)),
            dma((PARTS, 6)),
            dma((PARTS, 6)),
            dma((PARTS, 2, 4)),
            dma((PARTS, 2, 4)),
            dma((PARTS, 7)),
            dma((PARTS, 7)),
        ],
        compiler_params=pltpu.CompilerParams(
            collective_id=0, has_side_effects=True, vmem_limit_bytes=60 * 2**20
        ),
        cost_estimate=pl.CostEstimate(
            flops=2 * LISTED * tokens * BS * BS, bytes_accessed=4 * 2**20, transcendentals=tokens * COLS * BS
        ),
        name="block_grads",
    )(features, gate_pre, up_pre, grad_hidden, blocks.T, owner, owner.reshape(1, LISTED))
    is_valid = (jnp.arange(CAP, dtype=jnp.int32) < count[0])[:, None, None]
    first_new = beta_first * moment1 + (1.0 - beta_first) * block_grad
    second_new = beta_second * moment2 + (1.0 - beta_second) * block_grad * block_grad
    weight_new = weights - learn_rate * (first_new / bias_first) / (
        jnp.sqrt(second_new / bias_second) + epsilon
    )
    return (
        jnp.where(is_valid, weight_new, weights),
        jnp.where(is_valid, first_new, moment1),
        jnp.where(is_valid, second_new, moment2),
    )


def solution(mesh):
    tokens = P("dp", "tensor")
    state = P(("dp", "tensor"), None, None)
    return jax.shard_map(
        local,
        mesh=mesh,
        in_specs=(tokens,) * 4 + (P("tensor", None), P("tensor")) + (state,) * 3,
        out_specs=(state,) * 3,
        check_vma=False,
    )
```

```python
import functools

import jax
import jax.numpy as jnp
from jax import lax
from jax.experimental import pallas as pl
from jax.experimental.pallas import tpu as pltpu
from jax.sharding import PartitionSpec as P

beta_first = 0.9
beta_second = 0.999
learn_rate = 0.01
epsilon = 1e-08
bias_first = 1.0 - 0.9**10
bias_second = 1.0 - 0.999**10

NX, NY, NZ = 4, 8, 8
BS = 128
COLS = 14
CELLS = 8
LISTED = 64
CAP = 3
MESH = pl.DeviceIdType.MESH
PARTS = 4
ROWS = BS // PARTS
ORDER = (0, 1, 2, 0, 3, 1, 2, 0, 3, 1, 2, 0, 3, 1, 2, 0, 3, 1, 2, 3)
CHUNK = 4
PER = CELLS // CHUNK
RING = tuple(
    [(d, c) for d in range(3) for c in order] + [(3, c) for c in order[: PER // 2]]
    for order in (list(range(PER)), list(range(PER))[::-1])
)
HOPS = len(RING[0])
F32, BF16 = jnp.float32, jnp.bfloat16


def kernel(
    feat, gate, up, ghid, blk, own_s, own_v,
    bg_out, cnt_out,
    feats, gate_v, up_v, ghid_v, acts, table_v, table,
    send_c, recv_c, tot,
    x_two, x_in, x_one, x_fwd, x_left, x_right, part,
    y_out, y_in, gath,
    feat_sem, in_sem, table_sem, zs, zr, cs, cr, xs, xr, ys, yr, gs, gr,
):
    z = lax.axis_index("tensor")
    dp = lax.axis_index("dp")
    core = lax.rem(dp, 2)
    x = lax.rem(dp // 2, NX)
    y = dp // (2 * NX)

    def at(yy, xx, cc):
        return {"dp": (yy * NX + xx) * 2 + cc}

    def shift(v, by, n):
        return lax.rem(v + (by % n), n)

    zdev = ({"tensor": shift(z, 1, NZ)}, {"tensor": shift(z, -1, NZ)})
    xdev = {k: at(y, shift(x, k, NX), core) for k in (1, -1, 2)}
    ydev = {k: at(shift(y, k, NY), x, core) for k in (1, -1, 2, -2)}
    sib = at(y, x, 1 - core)

    in_copies = [
        pltpu.make_async_copy(s, d, in_sem.at[i])
        for i, (s, d) in enumerate(((gate, gate_v), (up, up_v), (ghid, ghid_v)))
    ]
    own_cells = [
        pltpu.make_async_copy(
            feat.at[:, pl.ds(BS * j, BS)], feats.at[z * CELLS + j], feat_sem.at[j]
        )
        for j in range(CELLS)
    ]
    for c in own_cells:
        c.start()
    for c in in_copies:
        c.start()

    barrier = pltpu.get_barrier_semaphore()
    partners = (*zdev, *xdev.values(), *ydev.values(), sib)
    for dev in partners:
        pl.semaphore_signal(barrier, inc=1, device_id=dev, device_id_type=MESH)
    pl.semaphore_wait(barrier, len(partners))

    def rcopy(src, dst, ssem, rsem, dev):
        return pltpu.make_async_remote_copy(
            src_ref=src, dst_ref=dst, send_sem=ssem, recv_sem=rsem,
            device_id=dev, device_id_type=MESH,
        )

    def ring(way, k, hop):
        dist, half = RING[way][k]
        src = shift(z, -(dist + hop) if way == 0 else dist + hop, NZ)
        cells = feats.at[pl.ds(src * CELLS + half * CHUNK, CHUNK)]
        return rcopy(cells, cells, zs.at[way, k], zr.at[way, k], zdev[way])

    for c in own_cells:
        c.wait()
    for k in range(PER):
        for way in (0, 1):
            ring(way, k, 0).start()

    owner_row = own_v[...] // (2 * NX)
    wide = jnp.broadcast_to(owner_row, (LISTED, LISTED))
    tall = wide.T
    lane = lax.broadcasted_iota(jnp.int32, (LISTED, LISTED), 1)
    sub = lax.broadcasted_iota(jnp.int32, (LISTED, LISTED), 0)
    rank_row = jnp.sum(
        ((tall < wide) | ((tall == wide) & (sub < lane))).astype(jnp.int32), axis=0, keepdims=True
    )
    rank_col = jnp.broadcast_to(rank_row, (LISTED, LISTED)).T
    order_row = jnp.sum(jnp.where(rank_col == lane, sub, 0), axis=0, keepdims=True)
    start_row = jnp.sum((tall < lane).astype(jnp.int32), axis=0, keepdims=True)
    table_v[...] = jnp.zeros_like(table_v)
    table_v[0:1, 0:LISTED] = order_row
    table_v[1:2, 0:LISTED] = rank_row
    table_v[2:3, 0:LISTED] = start_row
    to_smem = pltpu.make_async_copy(table_v, table, table_sem)
    to_smem.start()

    for c in in_copies:
        c.wait()

    def make_acts(c, carry):
        cols = pl.ds(pl.multiple_of(c * BS, BS), BS)
        g = gate_v[:, cols].astype(F32)
        h = ghid_v[:, cols].astype(F32)
        u = up_v[:, cols].astype(F32)
        s = jax.nn.sigmoid(g)
        d_up = (h * (g * s)).astype(BF16)
        d_gate = (h * u * (s * (1.0 + g * (1.0 - s)))).astype(BF16)
        acts[c] = d_gate.T
        acts[c + COLS] = d_up.T
        return carry

    done = 0
    for k in range(PER, HOPS):
        upto = min(COLS, (k - PER + 1) * COLS // (HOPS - PER - 1))
        if upto > done:
            lax.fori_loop(done, upto, make_acts, 0)
            done = upto
        for way in (0, 1):
            ring(way, k - PER, 1).wait_recv()
            ring(way, k, 0).start()
    to_smem.wait()

    def find(k, carry):
        count, q0, q1, q2 = carry
        mine = own_s[k] == dp
        q = table[1, k]
        q0 = jnp.where(mine & (count == 0), q, q0)
        q1 = jnp.where(mine & (count == 1), q, q1)
        q2 = jnp.where(mine & (count == 2), q, q2)
        return count + mine.astype(jnp.int32), q0, q1, q2

    zero = jnp.int32(0)
    count, *mine_at = lax.fori_loop(0, LISTED, find, (zero, zero, zero, zero))
    cnt_out[0] = count

    for k in range(HOPS - PER, HOPS):
        for way in (0, 1):
            ring(way, k, 1).wait_recv()

    def product(xx, cc, i):
        k = table[0, i * 8 + xx * 2 + cc]
        a = acts[blk[0, k] * COLS + blk[2, k]]
        return jnp.dot(a, feats[blk[1, k]], preferred_element_type=F32)

    def products(dst, n, xx, cc, places=range(8)):
        for i in places:
            dst[n, i] = product(xx, cc, i)

    rel = (2, 1, 3, 0)
    sent = []

    def send(*copy):
        c = rcopy(*copy)
        c.start()
        return c

    to_sib = {}

    def for_sib(n):
        xx = shift(x, rel[n], NX)
        for m in (0, 1) if n == 0 else (0,):
            places = slice(4 * m, 4 * m + 4) if n == 0 else slice(0, 8)
            products(send_c, n, xx, 1 - core, range(8)[places])
            part_c = pl.ds(places.start, places.stop - places.start)
            to_sib[n, m] = send(
                send_c.at[n, part_c], recv_c.at[n, part_c], cs.at[n, m], cr.at[n, m], sib
            )

    def for_me(n):
        products(tot, n, shift(x, rel[n], NX), core)

    def rows_of(h):
        return pl.ds(h * ROWS, ROWS)

    lo, hi = pl.ds(0, 4), pl.ds(4, 4)
    along_x = [{} for _ in range(PARTS)]

    def to_x(h, name, n, src, dst, step):
        along_x[h][name] = send(src, dst, xs.at[h, n], xr.at[h, n], xdev[step])

    def core_sum(n):
        if n > 0:
            to_sib[n, 0].wait_recv()
            tot[n] = tot[n] + recv_c[n]
            return
        for m, (places, step) in enumerate(((lo, 1), (hi, -1))):
            to_sib[0, m].wait_recv()
            for h in range(PARTS):
                x_two[h, places] = (tot[0, places, rows_of(h)] + recv_c[0, places, rows_of(h)]).astype(BF16)
                to_x(h, ("two+", "two-")[m], m, x_two.at[h, places], x_in.at[h, m], step)

    for_sib(0)
    for_sib(1)
    for_me(0)
    core_sum(0)
    for_sib(2)
    for_me(1)
    core_sum(1)
    for_me(2)
    core_sum(2)

    col = x * 2 + core

    def first_of(yy, column):
        return (table[2, yy] + (7 - column)) // 8

    def column(cc, h):
        return gath.at[pl.ds(cc * CAP, CAP), rows_of(h)]

    def tail(h):
        mine = rows_of(h)
        moves = along_x[h]
        x_one[h, 0] = tot[1, hi, mine].astype(BF16)
        to_x(h, "one+", 2, x_one.at[h, 0], x_left.at[h, hi], 1)
        x_one[h, 1] = tot[2, lo, mine].astype(BF16)
        to_x(h, "one-", 3, x_one.at[h, 1], x_right.at[h, lo], -1)
        yield
        moves["two+"].wait_recv()
        x_fwd[h, 0] = (tot[1, lo, mine] + x_in[h, 0].astype(F32)).astype(BF16)
        to_x(h, "fwd+", 4, x_fwd.at[h, 0], x_left.at[h, lo], 1)
        moves["two-"].wait_recv()
        x_fwd[h, 1] = (tot[2, hi, mine] + x_in[h, 1].astype(F32)).astype(BF16)
        to_x(h, "fwd-", 5, x_fwd.at[h, 1], x_right.at[h, hi], -1)
        yield
        for name in ("one+", "one-", "fwd+", "fwd-"):
            moves[name].wait_recv()
        part[:, mine] = tot[3, :, mine] + x_left[h].astype(F32) + x_right[h].astype(F32)

        def term(yy, e):
            return part[jnp.minimum(first_of(yy, col) + e, 7), mine]

        def along_y(way, kind, dist, hop, came=()):
            sign = 1 if way == 0 else -1
            yy = shift(y, sign * dist, NY)
            for e in range(CAP):
                v = term(yy, e)
                for k in came:
                    v = v + y_in[h, way, k, e].astype(F32)
                y_out[h, way, kind, e] = v.astype(BF16)
            return send(
                y_out.at[h, way, kind], y_in.at[h, way, kind],
                ys.at[h, way, kind], yr.at[h, way, kind], ydev[sign * hop],
            )

        far = h % 2
        ways = (far, 1 - far)
        third = {w: along_y(w, 0, 3, 1) for w in ways}
        fourth = along_y(far, 2, 4, 2)
        yield
        if h == 0:
            for k in range(HOPS):
                for way in (0, 1):
                    ring(way, k, 0).wait_send()
            for c in to_sib.values():
                c.wait_send()
        first, second = {}, {}
        for w in ways:
            third[w].wait_recv()
            if w == far:
                fourth.wait_recv()
            second[w] = along_y(w, 3, 2, 2, (0, 2) if w == far else (0,))
        for w in ways:
            first[w] = along_y(w, 1, 1, 1)
        yield
        for c in moves.values():
            c.wait_send()
        for w in ways:
            first[w].wait_recv()
            second[w].wait_recv()
        for e in range(CAP):
            v = term(y, e)
            for w in (0, 1):
                v = v + (y_in[h, w, 1, e].astype(F32) + y_in[h, w, 3, e].astype(F32))
            gath[col * CAP + e, mine] = v

        own = column(col, h)
        x_copy = [send(own, own, gs.at[h, n], gr.at[h, n], xdev[k]) for n, k in enumerate((2, 1, -1))]
        sib_copy = [send(own, own, gs.at[h, 3], gr.at[h, 3], sib)]
        yield
        for n, k in ((1, 1), (2, -1), (0, 2)):
            x_copy[n].wait_recv()
            came = column(shift(x, -k, NX) * 2 + core, h)
            sib_copy.append(send(came, came, gs.at[h, 4 + n], gr.at[h, 4 + n], sib))
        for c in (*third.values(), fourth, *first.values(), *second.values()):
            c.wait_send()
        yield
        for c in sib_copy:
            c.wait_recv()
        sent.extend((*x_copy, *sib_copy))

    turns = [tail(h) for h in range(PARTS)]
    next(turns[0])
    for_sib(3)
    for_me(3)
    next(turns[0])
    for turn in turns[1:]:
        next(turn)
        next(turn)
    core_sum(3)
    for h in ORDER:
        next(turns[h], None)

    for s in range(CAP):
        q = mine_at[s]
        column_of = lax.rem(q, 8)
        e = q // 8 - first_of(y, column_of)
        at_row = jnp.clip(column_of * CAP + e, 0, 8 * CAP - 1)
        bg_out[s] = gath[at_row].T

    for c in sent:
        c.wait_send()


def local(features, gate_pre, up_pre, grad_hidden, blocks, owner, weights, moment1, moment2):
    hbm = pl.BlockSpec(memory_space=pltpu.HBM)
    smem = pl.BlockSpec(memory_space=pltpu.SMEM)
    vmem = pl.BlockSpec(memory_space=pltpu.VMEM)
    tokens = features.shape[0]
    dma = pltpu.SemaphoreType.DMA
    block_grad, count = pl.pallas_call(
        kernel,
        out_shape=(
            jax.ShapeDtypeStruct((CAP, BS, BS), F32),
            jax.ShapeDtypeStruct((1,), jnp.int32),
        ),
        in_specs=[hbm, hbm, hbm, hbm, smem, smem, vmem],
        out_specs=(vmem, smem),
        scratch_shapes=[
            pltpu.VMEM((NZ * CELLS, tokens, BS), BF16),
            pltpu.VMEM(gate_pre.shape, BF16),
            pltpu.VMEM(gate_pre.shape, BF16),
            pltpu.VMEM(gate_pre.shape, BF16),
            pltpu.VMEM((2 * COLS, BS, tokens), BF16),
            pltpu.VMEM((8, 128), jnp.int32),
            pltpu.SMEM((8, 128), jnp.int32),
            pltpu.VMEM((4, 8, BS, BS), F32),
            pltpu.VMEM((4, 8, BS, BS), F32),
            pltpu.VMEM((4, 8, BS, BS), F32),
            pltpu.VMEM((PARTS, 8, ROWS, BS), BF16),
            pltpu.VMEM((PARTS, 2, 4, ROWS, BS), BF16),
            pltpu.VMEM((PARTS, 2, 4, ROWS, BS), BF16),
            pltpu.VMEM((PARTS, 2, 4, ROWS, BS), BF16),
            pltpu.VMEM((PARTS, 8, ROWS, BS), BF16),
            pltpu.VMEM((PARTS, 8, ROWS, BS), BF16),
            pltpu.VMEM((8, BS, BS), F32),
            pltpu.VMEM((PARTS, 2, 4, CAP, ROWS, BS), BF16),
            pltpu.VMEM((PARTS, 2, 4, CAP, ROWS, BS), BF16),
            pltpu.VMEM((8 * CAP, BS, BS), F32),
            dma((CELLS,)),
            dma((3,)),
            dma,
            dma((2, HOPS)),
            dma((2, HOPS)),
            dma((4, 2)),
            dma((4, 2)),
            dma((PARTS, 6)),
            dma((PARTS, 6)),
            dma((PARTS, 2, 4)),
            dma((PARTS, 2, 4)),
            dma((PARTS, 7)),
            dma((PARTS, 7)),
        ],
        compiler_params=pltpu.CompilerParams(
            collective_id=0, has_side_effects=True, vmem_limit_bytes=107 * 2**19
        ),
        cost_estimate=pl.CostEstimate(
            flops=2 * LISTED * tokens * BS * BS, bytes_accessed=4 * 2**20, transcendentals=tokens * COLS * BS
        ),
        name="block_grads",
    )(features, gate_pre, up_pre, grad_hidden, blocks.T, owner, owner.reshape(1, LISTED))
    is_valid = (jnp.arange(CAP, dtype=jnp.int32) < count[0])[:, None, None]
    first_new = beta_first * moment1 + (1.0 - beta_first) * block_grad
    second_new = beta_second * moment2 + (1.0 - beta_second) * block_grad * block_grad
    weight_new = weights - learn_rate * (first_new / bias_first) / (
        jnp.sqrt(second_new / bias_second) + epsilon
    )
    return (
        jnp.where(is_valid, weight_new, weights),
        jnp.where(is_valid, first_new, moment1),
        jnp.where(is_valid, second_new, moment2),
    )


def solution(mesh):
    tokens = P("dp", "tensor")
    state = P(("dp", "tensor"), None, None)
    return jax.shard_map(
        local,
        mesh=mesh,
        in_specs=(tokens,) * 4 + (P("tensor", None), P("tensor")) + (state,) * 3,
        out_specs=(state,) * 3,
        check_vma=False,
    )
```
